32 devices in a mesh: seq: 8 (over z, core), kvh: 2 (over x), batch: 2 (over y).
Axes of the slice: x: 2, y: 2, z: 4, core: 2. Of those that a mesh axis runs over, the one named last changes fastest.
Arguments:
- query: bfloat16 [2048, 1280], P(('batch', 'seq'), 'kvh'), parts along dimension 0, may hold values from -33.3 to 33.3
- self_keys: bfloat16 [2048, 256], P(('batch', 'seq'), 'kvh'), parts along dimension 0, may hold values from -6.4 to 6.4
- self_values: bfloat16 [2048, 256], P(('batch', 'seq'), 'kvh'), parts along dimension 0, may hold values from -6 to 6
- cache_keys: bfloat16 [8192, 256], P(('batch', 'seq'), 'kvh'), parts along dimension 0, may hold values from -6.375 to 6.375
- cache_values: bfloat16 [8192, 256], P(('batch', 'seq'), 'kvh'), parts along dimension 0, may hold values from -6 to 6
- cache_pos: int32 [8192], P(('batch', 'seq')), parts along dimension 0, may hold values from 0 to 4095, each once
- d_out: bfloat16 [2048, 1280], P(('batch', 'seq'), 'kvh'), parts along dimension 0, may hold values from -6 to 6
Outputs:
- attended: bfloat16 [2048, 1280], P(('batch', 'seq'), 'kvh'), parts along dimension 0
- grad_query: bfloat16 [2048, 1280], P(('batch', 'seq'), 'kvh'), parts along dimension 0
- grad_keys: bfloat16 [2048, 256], P(('batch', 'seq'), 'kvh'), parts along dimension 0
- grad_values: bfloat16 [2048, 256], P(('batch', 'seq'), 'kvh'), parts along dimension 0
The draws below stay inside these ranges and needn't reach their ends.
There are 2 independent parts, one for each index of `batch`. The reference program is written for one: setup_inputs(seed, part) draws one part's arguments, and reference() takes and returns one part's arrays. A program takes and returns all parts, laid end to end along the dimension named above; each array names one. Nothing has to cross between parts.
Inputs may be any that keep to these rules, and one draw needn't show every extreme that they name: `cache_pos`: each cache position appears once.
All inputs are finite; a program needn't handle non-finite values.
Results may differ from the reference program's by a relative error of at most 0.012.
The reference program's roundings to bfloat16 on the way count: a program that leaves them out, or rounds other values in their place, can miss the bound.
Values may be sent and summed in bfloat16 or wider, within the bound.
A program may use at most 64 MiB of HBM per device.

```python
import jax
import jax.numpy as jnp
from jax import lax

HD = 128
GROUP = 5
WINDOW = 512
KV_HEADS = 2
Q_HEADS = 10
TOKENS = 1024
CACHED = 4096


def shared_draw(key):
    base = jax.random.fold_in(key, 907)
    seed_keys, seed_queries = jax.random.split(base, 2)
    key_rows = jnp.clip(jax.random.normal(seed_keys, (TOKENS, KV_HEADS, HD), jnp.float32) * 1.6, -6.375, 6.375)
    query_rows = jnp.clip(jax.random.normal(seed_queries, (TOKENS, KV_HEADS, GROUP, HD), jnp.float32) * 1.6, -6.375, 6.375)
    return (key_rows, query_rows)


def draw_query(key, part):
    key_rows, query_rows = shared_draw(key)
    return query_rows.reshape(TOKENS, KV_HEADS * GROUP * HD).astype(jnp.bfloat16)


def draw_self_keys(key, part):
    key_rows, query_rows = shared_draw(key)
    return key_rows.reshape(TOKENS, KV_HEADS * HD).astype(jnp.bfloat16)


def levels(own_key, dims, cuts, low, largest):
    def one(position, shards_of):
        heights = jax.random.uniform(jax.random.fold_in(jax.random.fold_in(own_key, 6), position), (shards_of,), jnp.float32, low / len(cuts), largest / len(cuts))
        return jnp.repeat(jnp.exp(heights), dims[position] // shards_of).reshape((-1,) + (1,) * (len(dims) - position - 1))

    factor_of = one(*cuts[0])
    for cut in cuts[1:]:
        factor_of = factor_of * one(*cut)
    return factor_of


def centred(stream_key, extent, deviation, reach, cuts=(), kind=jnp.bfloat16):
    drawn = deviation * jax.random.normal(stream_key, extent, jnp.float32)
    if cuts:
        drawn = drawn * levels(stream_key, extent, cuts, -0.22, 0.18)
    return jnp.clip(drawn, -reach, reach).astype(kind)


def setup_inputs(seed: int = 0, part: int = 0) -> dict:
    key_of = jax.random.split(jax.random.key(seed), 8)
    part_splits = jax.random.split(jax.random.fold_in(key_of[7], part), 8)
    return {
        "query": draw_query(jax.random.fold_in(jax.random.fold_in(key_of[7], part), 71), part),
        "self_keys": draw_self_keys(jax.random.fold_in(jax.random.fold_in(key_of[7], part), 71), part),
        "self_values": centred(part_splits[2], (TOKENS, KV_HEADS * HD), 1.0, 6.0, ((0, 8), (1, 2))),
        "cache_keys": centred(part_splits[3], (CACHED, KV_HEADS * HD), 1.6, 6.375, ((0, 8), (1, 2))),
        "cache_values": centred(part_splits[4], (CACHED, KV_HEADS * HD), 1.0, 6.0, ((0, 8), (1, 2))),
        "cache_pos": jax.random.permutation(part_splits[5], CACHED).astype(jnp.int32),
        "d_out": centred(part_splits[6], (TOKENS, Q_HEADS * HD), 1.0, 6.0, ((0, 8), (1, 2))),
    }


row_block = 64


def reference(query, self_keys, self_values, cache_keys, cache_values, cache_pos, d_out):
    scaling = HD ** -0.5
    start_pos = CACHED - TOKENS
    key_all = jnp.concatenate([cache_keys, self_keys], axis=0).astype(jnp.float32).reshape(CACHED + TOKENS, KV_HEADS, HD)
    value_all = jnp.concatenate([cache_values, self_values], axis=0).astype(jnp.float32).reshape(CACHED + TOKENS, KV_HEADS, HD)
    query_all = query.astype(jnp.float32).reshape(TOKENS, KV_HEADS, GROUP, HD)
    grads_all = d_out.astype(jnp.float32).reshape(TOKENS, KV_HEADS, GROUP, HD)
    self_index = jnp.arange(TOKENS, dtype=jnp.int32)

    def one_block(carried, block_no):
        key_acc, value_acc = carried
        first_row = (block_no * row_block).astype(jnp.int32)
        row_index = first_row + jnp.arange(row_block, dtype=jnp.int32)
        queries = lax.dynamic_slice_in_dim(query_all, first_row, row_block, 0)
        grads_out = lax.dynamic_slice_in_dim(grads_all, first_row, row_block, 0)
        bound_pos = start_pos + jnp.maximum(row_index - WINDOW + 1, 0)
        cache_vis = cache_pos[None, :] < bound_pos[:, None]
        self_vis = (self_index[None, :] <= row_index[:, None]) & (self_index[None, :] >= row_index[:, None] - WINDOW + 1)
        visible = jnp.concatenate([cache_vis, self_vis], axis=1)
        scores = jnp.einsum("tkgd,ckd->kgtc", queries, key_all) * scaling
        scores = jnp.where(visible[None, None], scores, -jnp.inf)
        row_max = jnp.max(scores, axis=-1, keepdims=True)
        log_total = row_max + jnp.log(jnp.sum(jnp.exp(scores - row_max), axis=-1, keepdims=True))
        weights = jnp.exp(scores - log_total)
        rounded = lax.optimization_barrier(weights.astype(jnp.bfloat16)).astype(jnp.float32)
        outputs = jnp.einsum("kgtc,ckd->tkgd", rounded, value_all)
        attended = outputs.astype(jnp.bfloat16)
        attended_wide = lax.optimization_barrier(attended).astype(jnp.float32)
        delta_rows = jnp.sum(grads_out * attended_wide, axis=-1)
        grad_weights = jnp.einsum("tkgd,ckd->kgtc", grads_out, value_all)
        grad_scores = weights * (grad_weights - jnp.transpose(delta_rows, (1, 2, 0))[..., None])
        grad_round = lax.optimization_barrier(grad_scores.astype(jnp.bfloat16)).astype(jnp.float32)
        grad_query = (jnp.einsum("kgtc,ckd->tkgd", grad_round, key_all) * scaling).astype(jnp.bfloat16)
        key_acc = key_acc + jnp.einsum("kgtc,tkgd->ckd", grad_round[..., CACHED:], queries)
        value_acc = value_acc + jnp.einsum("kgtc,tkgd->ckd", rounded[..., CACHED:], grads_out)
        return (key_acc, value_acc), (attended.reshape(row_block, Q_HEADS * HD), grad_query.reshape(row_block, Q_HEADS * HD))

    empty = jnp.zeros((TOKENS, KV_HEADS, HD), jnp.float32)
    (key_acc, value_acc), (attended_blocks, query_blocks) = lax.scan(one_block, (empty, empty), jnp.arange(TOKENS // row_block, dtype=jnp.int32))
    attended = attended_blocks.reshape(TOKENS, Q_HEADS * HD)
    grad_query = query_blocks.reshape(TOKENS, Q_HEADS * HD)
    grad_keys = (key_acc * scaling).astype(jnp.bfloat16).reshape(TOKENS, KV_HEADS * HD)
    grad_values = value_acc.astype(jnp.bfloat16).reshape(TOKENS, KV_HEADS * HD)
    return (attended, grad_query, grad_keys, grad_values)
```

```python
import functools
import math

import jax
import jax.numpy as jnp
from jax import lax
from jax.experimental import pallas as pl
from jax.experimental.pallas import tpu as pltpu
from jax.sharding import PartitionSpec as P

HD = 128
GROUP = 5
WINDOW = 512
NEG = -1e30
F32 = jnp.float32
BF16 = jnp.bfloat16
MESH = pl.DeviceIdType.MESH

LAST = (((1,), (1,)), ((), ()))
FIRST = (((0,), (0,)), ((), ()))


def dot_nt(a, b):
    return lax.dot_general(a, b, LAST, preferred_element_type=F32)


def dot_tn(a, b):
    return lax.dot_general(a, b, FIRST, preferred_element_type=F32)


def dot_nn(a, b):
    return jnp.dot(a, b, preferred_element_type=F32)


def lane_tiles(x, op):
    parts = [x[:, i : i + 128] for i in range(0, x.shape[1], 128)]
    return functools.reduce(op, parts)


def kernel(
    n, q_ref, sk_ref, sv_ref, ck_ref, cv_ref, cp_ref, do_ref,
    att_ref, dq_ref, dk_ref, dv_ref,
    qs, ds_out, kbuf, vbuf, pos, s_ref, dp_ref, sw_ref, m_ref, l_ref, acc,
    gk_send, gv_send, gk_recv, gv_recv,
    send_sem, recv_sem, pos_send, pos_recv, g_send, g_recv,
):
    rows = q_ref.shape[0]
    cached = ck_ref.shape[0]
    rim = (WINDOW + rows - 2) // rows
    rim_chips = (rim + 1) // 2
    chips = n // 2
    start_pos = (cached - rows) * n
    scale = HD ** -0.5
    scale2 = scale * math.log2(math.e)

    me = lax.axis_index("seq")
    z = me // 2
    core = me % 2
    sib = z * 2 + (1 - core)

    bufs = (kbuf, vbuf)
    kbuf[me, 0:cached] = ck_ref[...]
    kbuf[me, cached:] = sk_ref[...]
    vbuf[me, 0:cached] = cv_ref[...]
    vbuf[me, cached:] = sv_ref[...]
    pos[me] = cp_ref[...]

    barrier = pltpu.get_barrier_semaphore()
    for k in range(1, n):
        pl.semaphore_signal(
            barrier, inc=1, device_id={"seq": (me + k) % n}, device_id_type=MESH
        )
    pl.semaphore_wait(barrier, n - 1)

    def block_copy(a, way, o, size, target):
        part = bufs[a].at[o, pl.ds(0, size)]
        return pltpu.make_async_remote_copy(
            src_ref=part,
            dst_ref=part,
            send_sem=send_sem.at[a, way, o],
            recv_sem=recv_sem.at[a, o],
            device_id={"seq": target},
            device_id_type=MESH,
        )

    full = cached + rows

    def sized(near, run):
        @pl.when(near)
        def _():
            run(full)

        @pl.when(jnp.logical_not(near))
        def _():
            run(cached)

    def relay(a, t, act):
        left = me - 2 * t
        right = me + 2 * t

        def push(way, o, size, target):
            copy = block_copy(a, way, o, size, target)
            if act == "go":
                copy.start()
            else:
                copy.wait_send()

        @pl.when(z - t >= 0)
        def _():
            if act == "go":
                @pl.when(t > 0)
                def _():
                    sized(t <= rim_chips, lambda size: block_copy(a, 0, left, size, sib).wait_recv())

            @pl.when(z < chips - 1)
            def _():
                sized(t + 1 <= rim_chips, lambda size: push(0, left, size, me + 2))

            @pl.when(t == 0)
            def _():
                @pl.when(z > 0)
                def _():
                    push(1, left, cached, me - 2)

            sized(t <= rim_chips, lambda size: push(2, left, size, sib))

        @pl.when((t > 0) & (z + t < chips))
        def _():
            if act == "go":
                block_copy(a, 1, right, cached, sib).wait_recv()

            @pl.when(z > 0)
            def _():
                push(1, right, cached, me - 2)

            push(2, right, cached, sib)

    def consume(a, t, use):
        left = me - 2 * t
        right = me + 2 * t
        left_sib = left + sib - me
        right_sib = right + sib - me

        @pl.when(z - t >= 0)
        def _():
            use(left)

        @pl.when((t > 0) & (z + t < chips))
        def _():
            use(right)

        @pl.when(z - t >= 0)
        def _():
            sized(t <= rim_chips, lambda size: block_copy(a, 0, left_sib, size, sib).wait_recv())
            use(left_sib)

        @pl.when((t > 0) & (z + t < chips))
        def _():
            block_copy(a, 0, right_sib, cached, sib).wait_recv()
            use(right_sib)

    def pos_copy(o, target):
        return pltpu.make_async_remote_copy(
            src_ref=pos.at[o],
            dst_ref=pos.at[o],
            send_sem=pos_send.at[target],
            recv_sem=pos_recv.at[o],
            device_id={"seq": target},
            device_id_type=MESH,
        )

    relay(0, 0, "go")
    for k in range(1, n):
        pos_copy(me, (me + k) % n).start()

    def head(g):
        return slice(g * rows, (g + 1) * rows)

    for g in range(GROUP):
        qs[head(g)] = q_ref[:, g * HD : (g + 1) * HD]
        ds_out[head(g)] = do_ref[:, g * HD : (g + 1) * HD]
    m_ref[...] = jnp.full(m_ref.shape, NEG, F32)
    l_ref[...] = jnp.zeros(l_ref.shape, F32)
    acc[...] = jnp.zeros(acc.shape, F32)

    row_index = me * rows + lax.broadcasted_iota(jnp.int32, (rows, 1), 0)
    bound = start_pos + jnp.maximum(row_index - WINDOW + 1, 0)

    def score_shard(o):
        @pl.when(o != me)
        def _():
            pos_copy(o, sib).wait_recv()

        vis = pos[o] < bound
        for g in range(GROUP):
            s = dot_nt(qs[head(g)], kbuf[o, 0:cached])
            s = jnp.where(vis, s, NEG)
            s_ref[o, head(g)] = s
            m_ref[head(g)] = jnp.maximum(m_ref[head(g)], lane_tiles(s, jnp.maximum))

    @pl.loop(0, chips)
    def _(t):
        @pl.when(t > 0)
        def _():
            relay(0, t, "go")

        @pl.when(t == 1)
        def _():
            relay(1, 0, "go")

        consume(0, t, score_shard)

    first = jnp.maximum(me - rim, 0)
    delta_index = lax.broadcasted_iota(jnp.int32, (rows, rows), 0) - lax.broadcasted_iota(
        jnp.int32, (rows, rows), 1
    )

    @pl.loop(first, me + 1)
    def _(o):
        d = me - o
        gap = delta_index + d * rows
        vis = (gap >= 0) & (gap < WINDOW)
        for g in range(GROUP):
            s = dot_nt(qs[head(g)], kbuf[o, cached:])
            s = jnp.where(vis, s, NEG)
            sw_ref[d, head(g)] = s
            m_ref[head(g)] = jnp.maximum(m_ref[head(g)], s)

    for g in range(GROUP):
        top = jnp.max(m_ref[head(g)], axis=1, keepdims=True)
        m_ref[head(g)] = jnp.broadcast_to(top, (rows, 128))

    @pl.loop(0, n)
    def _(o):
        for g in range(GROUP):
            p = jnp.exp2((s_ref[o, head(g)] - m_ref[head(g), 0:1]) * scale2)
            s_ref[o, head(g)] = p
            l_ref[head(g)] += lane_tiles(p, jnp.add)

    @pl.loop(first, me + 1)
    def _(o):
        d = me - o
        for g in range(GROUP):
            p = jnp.exp2((sw_ref[d, head(g)] - m_ref[head(g)]) * scale2)
            sw_ref[d, head(g)] = p
            l_ref[head(g)] += p

    for g in range(GROUP):
        total = jnp.sum(l_ref[head(g)], axis=1, keepdims=True)
        l_ref[head(g)] = jnp.broadcast_to(1.0 / total, (rows, 128))

    def grad_copy(a, d, target):
        sent, got = ((gk_send, gk_recv), (gv_send, gv_recv))[a]
        return pltpu.make_async_remote_copy(
            src_ref=sent.at[d],
            dst_ref=got.at[d],
            send_sem=g_send.at[a, d],
            recv_sem=g_recv.at[a, d],
            device_id={"seq": target},
            device_id_type=MESH,
        )

    @pl.loop(first, me + 1)
    def _(o):
        d = me - o
        total = jnp.zeros((rows, HD), F32)
        for g in range(GROUP):
            w = sw_ref[d, head(g)] * l_ref[head(g)]
            sw_ref[d, head(g)] = w
            total = total + dot_tn(w.astype(BF16), ds_out[head(g)])
        gv_send[d] = total.astype(BF16)

        @pl.when(d == 0)
        def _():
            dv_ref[...] = total

        @pl.when(d > 0)
        def _():
            grad_copy(1, d, o).start()

    def value_shard(o):
        v = vbuf[o, 0:cached]
        for g in range(GROUP):
            w = s_ref[o, head(g)] * l_ref[head(g), 0:1]
            acc[head(g)] += dot_nn(w.astype(BF16), v)
            dp_ref[o, head(g)] = dot_nt(ds_out[head(g)], v)

    @pl.loop(0, chips)
    def _(t):
        @pl.when(t > 0)
        def _():
            relay(1, t, "go")

        consume(1, t, value_shard)

    @pl.loop(first, me + 1)
    def _(o):
        d = me - o
        v = vbuf[o, cached:]
        for g in range(GROUP):
            acc[head(g)] += dot_nn(sw_ref[d, head(g)].astype(BF16), v)

    for g in range(GROUP):
        out = acc[head(g)].astype(BF16)
        att_ref[:, g * HD : (g + 1) * HD] = out
        delta = jnp.sum(ds_out[head(g)].astype(F32) * out.astype(F32), axis=1, keepdims=True)
        m_ref[head(g)] = jnp.broadcast_to(delta, (rows, 128))
    acc[...] = jnp.zeros(acc.shape, F32)

    @pl.loop(first, me + 1)
    def _(o):
        d = me - o
        v = vbuf[o, cached:]
        key = kbuf[o, cached:]
        total = jnp.zeros((rows, HD), F32)
        for g in range(GROUP):
            dp = dot_nt(ds_out[head(g)], v)
            gs = (sw_ref[d, head(g)] * (dp - m_ref[head(g)])).astype(BF16)
            total = total + dot_tn(gs, qs[head(g)])
            acc[head(g)] += dot_nn(gs, key)
        gk_send[d] = total.astype(BF16)

        @pl.when(d == 0)
        def _():
            dk_ref[...] = total

        @pl.when(d > 0)
        def _():
            grad_copy(0, d, o).start()

    @pl.loop(0, n)
    def _(o):
        key = kbuf[o, 0:cached]
        for g in range(GROUP):
            w = s_ref[o, head(g)] * l_ref[head(g), 0:1]
            gs = (w * (dp_ref[o, head(g)] - m_ref[head(g), 0:1])).astype(BF16)
            acc[head(g)] += dot_nn(gs, key)

    for g in range(GROUP):
        dq_ref[:, g * HD : (g + 1) * HD] = (acc[head(g)] * scale).astype(BF16)

    @pl.loop(0, chips)
    def _(t):
        relay(0, t, "end")
        relay(1, t, "end")

    for k in range(1, n):
        pos_copy(me, (me + k) % n).wait_send()

    for d in range(1, rim + 1):
        @pl.when(me - d >= 0)
        def _():
            grad_copy(1, d, sib).wait_send()
            grad_copy(0, d, sib).wait_send()

        @pl.when(me + d < n)
        def _():
            grad_copy(1, d, sib).wait_recv()
            grad_copy(0, d, sib).wait_recv()
            dk_ref[...] += gk_recv[d].astype(F32)
            dv_ref[...] += gv_recv[d].astype(F32)


def local(query, self_keys, self_values, cache_keys, cache_values, cache_pos, d_out):
    n = lax.axis_size("seq")
    rows = query.shape[0]
    cached = cache_keys.shape[0]
    rim = (WINDOW + rows - 2) // rows
    stacked = GROUP * rows
    vmem = pl.BlockSpec(memory_space=pltpu.VMEM)
    att, dq, dk, dv = pl.pallas_call(
        functools.partial(kernel, n),
        out_shape=(
            jax.ShapeDtypeStruct((rows, GROUP * HD), BF16),
            jax.ShapeDtypeStruct((rows, GROUP * HD), BF16),
            jax.ShapeDtypeStruct((rows, HD), F32),
            jax.ShapeDtypeStruct((rows, HD), F32),
        ),
        in_specs=[vmem] * 7,
        out_specs=(vmem,) * 4,
        scratch_shapes=[
            pltpu.VMEM((stacked, HD), BF16),
            pltpu.VMEM((stacked, HD), BF16),
            pltpu.VMEM((n, cached + rows, HD), BF16),
            pltpu.VMEM((n, cached + rows, HD), BF16),
            pltpu.VMEM((n, 1, cached), jnp.int32),
            pltpu.VMEM((n, stacked, cached), F32),
            pltpu.VMEM((n, stacked, cached), F32),
            pltpu.VMEM((rim + 1, stacked, rows), F32),
            pltpu.VMEM((stacked, 128), F32),
            pltpu.VMEM((stacked, 128), F32),
            pltpu.VMEM((stacked, HD), F32),
            pltpu.VMEM((rim + 1, rows, HD), BF16),
            pltpu.VMEM((rim + 1, rows, HD), BF16),
            pltpu.VMEM((rim + 1, rows, HD), BF16),
            pltpu.VMEM((rim + 1, rows, HD), BF16),
            pltpu.SemaphoreType.DMA((2, 3, n)),
            pltpu.SemaphoreType.DMA((2, n)),
            pltpu.SemaphoreType.DMA((n,)),
            pltpu.SemaphoreType.DMA((n,)),
            pltpu.SemaphoreType.DMA((2, rim + 1)),
            pltpu.SemaphoreType.DMA((2, rim + 1)),
        ],
        compiler_params=pltpu.CompilerParams(
            collective_id=0, has_side_effects=True, vmem_limit_bytes=56 * 2**20
        ),
    )(
        query, self_keys, self_values, cache_keys, cache_values,
        cache_pos.reshape(1, cached), d_out,
    )
    return att, dq, (dk * HD ** -0.5).astype(BF16), dv.astype(BF16)


def solution(mesh):
    split = P(("batch", "seq"), "kvh")
    return jax.shard_map(
        local,
        mesh=mesh,
        in_specs=(split, split, split, split, split, P(("batch", "seq")), split),
        out_specs=(split, split, split, split),
        check_vma=False,
    )
```

```python
import functools
import math

import jax
import jax.numpy as jnp
from jax import lax
from jax.experimental import pallas as pl
from jax.experimental.pallas import tpu as pltpu
from jax.sharding import PartitionSpec as P

HD = 128
GROUP = 5
WINDOW = 512
NEG = -1e30
F32 = jnp.float32
BF16 = jnp.bfloat16
MESH = pl.DeviceIdType.MESH

LAST = (((1,), (1,)), ((), ()))
FIRST = (((0,), (0,)), ((), ()))


def dot_nt(a, b):
    return lax.dot_general(a, b, LAST, preferred_element_type=F32)


def dot_tn(a, b):
    return lax.dot_general(a, b, FIRST, preferred_element_type=F32)


def dot_nn(a, b):
    return jnp.dot(a, b, preferred_element_type=F32)


def lane_tiles(x, op):
    parts = [x[:, i : i + 128] for i in range(0, x.shape[1], 128)]
    return functools.reduce(op, parts)


def kernel(
    n, q_ref, sk_ref, sv_ref, ck_ref, cv_ref, cp_ref, do_ref,
    att_ref, dq_ref, dk_ref, dv_ref,
    qs, ds_out, kbuf, vbuf, pos, s_ref, dp_ref, sw_ref, dw_ref, m_ref, l_ref, acc, own_k, own_v,
    gk_send, gv_send, gk_recv, gv_recv,
    send_sem, recv_sem, pos_send, pos_recv, g_send, g_recv,
):
    rows = q_ref.shape[0]
    cached = ck_ref.shape[0]
    rim = (WINDOW + rows - 2) // rows
    rim_chips = (rim + 1) // 2
    chips = n // 2
    start_pos = (cached - rows) * n
    scale = HD ** -0.5
    scale2 = scale * math.log2(math.e)

    me = lax.axis_index("seq")
    z = me // 2
    core = me % 2
    sib = z * 2 + (1 - core)

    bufs = (kbuf, vbuf)
    kbuf[me, 0:cached] = ck_ref[...]
    kbuf[me, cached:] = sk_ref[...]
    vbuf[me, 0:cached] = cv_ref[...]
    vbuf[me, cached:] = sv_ref[...]
    pos[me] = cp_ref[...]

    barrier = pltpu.get_barrier_semaphore()
    for k in range(1, n):
        pl.semaphore_signal(
            barrier, inc=1, device_id={"seq": (me + k) % n}, device_id_type=MESH
        )
    pl.semaphore_wait(barrier, n - 1)

    def block_copy(a, way, o, size, target):
        part = bufs[a].at[o, pl.ds(0, size)]
        return pltpu.make_async_remote_copy(
            src_ref=part,
            dst_ref=part,
            send_sem=send_sem.at[a, way, o],
            recv_sem=recv_sem.at[a, o],
            device_id={"seq": target},
            device_id_type=MESH,
        )

    full = cached + rows

    def sized(near, run):
        @pl.when(near)
        def _():
            run(full)

        @pl.when(jnp.logical_not(near))
        def _():
            run(cached)

    def relay(a, t, act):
        left = me - 2 * t
        right = me + 2 * t

        def push(way, o, size, target):
            copy = block_copy(a, way, o, size, target)
            if act == "go":
                copy.start()
            else:
                copy.wait_send()

        @pl.when(z - t >= 0)
        def _():
            if act == "go":
                @pl.when(t > 0)
                def _():
                    sized(t <= rim_chips, lambda size: block_copy(a, 0, left, size, sib).wait_recv())

            @pl.when(z < chips - 1)
            def _():
                sized(t + 1 <= rim_chips, lambda size: push(0, left, size, me + 2))

            @pl.when(t == 0)
            def _():
                @pl.when(z > 0)
                def _():
                    push(1, left, cached, me - 2)

            sized(t <= rim_chips, lambda size: push(2, left, size, sib))

        @pl.when((t > 0) & (z + t < chips))
        def _():
            if act == "go":
                block_copy(a, 1, right, cached, sib).wait_recv()

            @pl.when(z > 0)
            def _():
                push(1, right, cached, me - 2)

            push(2, right, cached, sib)

    def consume(a, t, use):
        left = me - 2 * t
        right = me + 2 * t
        left_sib = left + sib - me
        right_sib = right + sib - me

        @pl.when(z - t >= 0)
        def _():
            use(left)

        @pl.when((t > 0) & (z + t < chips))
        def _():
            use(right)

        @pl.when(z - t >= 0)
        def _():
            sized(t <= rim_chips, lambda size: block_copy(a, 0, left_sib, size, sib).wait_recv())
            use(left_sib)

        @pl.when((t > 0) & (z + t < chips))
        def _():
            block_copy(a, 0, right_sib, cached, sib).wait_recv()
            use(right_sib)

    def pos_copy(o, target):
        return pltpu.make_async_remote_copy(
            src_ref=pos.at[o],
            dst_ref=pos.at[o],
            send_sem=pos_send.at[target],
            recv_sem=pos_recv.at[o],
            device_id={"seq": target},
            device_id_type=MESH,
        )

    relay(0, 0, "go")
    for k in range(1, n):
        pos_copy(me, (me + k) % n).start()

    def head(g):
        return slice(g * rows, (g + 1) * rows)

    for g in range(GROUP):
        qs[head(g)] = q_ref[:, g * HD : (g + 1) * HD]
        ds_out[head(g)] = do_ref[:, g * HD : (g + 1) * HD]
    m_ref[...] = jnp.full(m_ref.shape, NEG, F32)
    l_ref[...] = jnp.zeros(l_ref.shape, F32)
    acc[...] = jnp.zeros(acc.shape, F32)

    row_index = me * rows + lax.broadcasted_iota(jnp.int32, (rows, 1), 0)
    bound = start_pos + jnp.maximum(row_index - WINDOW + 1, 0)

    def score_shard(o):
        @pl.when(o != me)
        def _():
            pos_copy(o, sib).wait_recv()

        vis = pos[o] < bound
        for g in range(GROUP):
            s = dot_nt(qs[head(g)], kbuf[o, 0:cached])
            s = jnp.where(vis, s, NEG)
            s_ref[o, head(g)] = s
            m_ref[head(g)] = jnp.maximum(m_ref[head(g)], lane_tiles(s, jnp.maximum))

    first = jnp.maximum(me - rim, 0)
    near_end = min(rim_chips, chips - 1)
    delta_index = lax.broadcasted_iota(jnp.int32, (rows, rows), 0) - lax.broadcasted_iota(
        jnp.int32, (rows, rows), 1
    )

    def window_scores():
        @pl.loop(first, me + 1)
        def _(o):
            d = me - o
            gap = delta_index + d * rows
            vis = (gap >= 0) & (gap < WINDOW)
            s = dot_nt(qs[...], kbuf[o, cached:])
            s = jnp.concatenate([jnp.where(vis, s[head(g)], NEG) for g in range(GROUP)], axis=0)
            sw_ref[d] = s
            m_ref[...] = jnp.maximum(m_ref[...], s)

    def window_values():
        @pl.loop(first, me + 1)
        def _(o):
            d = me - o
            v = vbuf[o, cached:]
            acc[...] += dot_nn(sw_ref[d].astype(BF16), v)
            dw_ref[d] = dot_nt(ds_out[...], v)

    @pl.loop(0, chips)
    def _(t):
        @pl.when(t > 0)
        def _():
            relay(0, t, "go")

        consume(0, t, score_shard)

        @pl.when(t > 0)
        def _():
            relay(1, t - 1, "go")

        @pl.when(t == near_end)
        def _():
            window_scores()

    for g in range(GROUP):
        top = jnp.max(m_ref[head(g)], axis=1, keepdims=True)
        m_ref[head(g)] = jnp.broadcast_to(top, (rows, 128))

    @pl.loop(0, n)
    def _(o):
        for g in range(GROUP):
            p = jnp.exp2((s_ref[o, head(g)] - m_ref[head(g), 0:1]) * scale2)
            s_ref[o, head(g)] = p
            l_ref[head(g)] += lane_tiles(p, jnp.add)

    @pl.loop(first, me + 1)
    def _(o):
        d = me - o
        p = jnp.exp2((sw_ref[d] - m_ref[...]) * scale2)
        sw_ref[d] = p
        l_ref[...] += p

    for g in range(GROUP):
        total = jnp.sum(l_ref[head(g)], axis=1, keepdims=True)
        l_ref[head(g)] = jnp.broadcast_to(1.0 / total, (rows, 128))

    def grad_copy(a, d, target):
        sent, got = ((gk_send, gk_recv), (gv_send, gv_recv))[a]
        return pltpu.make_async_remote_copy(
            src_ref=sent.at[d],
            dst_ref=got.at[d],
            send_sem=g_send.at[a, d],
            recv_sem=g_recv.at[a, d],
            device_id={"seq": target},
            device_id_type=MESH,
        )

    @pl.loop(first, me + 1)
    def _(o):
        d = me - o
        w = sw_ref[d] * l_ref[...]
        sw_ref[d] = w
        total = dot_tn(w.astype(BF16), ds_out[...])
        gv_send[d] = total.astype(BF16)

        @pl.when(d == 0)
        def _():
            own_v[...] = total

        @pl.when(d > 0)
        def _():
            grad_copy(1, d, o).start()

    def value_shard(o):
        v = vbuf[o, 0:cached]
        for g in range(GROUP):
            w = s_ref[o, head(g)] * l_ref[head(g), 0:1]
            acc[head(g)] += dot_nn(w.astype(BF16), v)
            dp_ref[o, head(g)] = dot_nt(ds_out[head(g)], v)

    @pl.loop(0, chips)
    def _(t):
        @pl.when(t == chips - 1)
        def _():
            relay(1, t, "go")

        consume(1, t, value_shard)

        @pl.when(t == near_end)
        def _():
            window_values()

    for g in range(GROUP):
        out = acc[head(g)].astype(BF16)
        att_ref[:, g * HD : (g + 1) * HD] = out
        delta = jnp.sum(ds_out[head(g)].astype(F32) * out.astype(F32), axis=1, keepdims=True)
        m_ref[head(g)] = jnp.broadcast_to(delta, (rows, 128))
    acc[...] = jnp.zeros(acc.shape, F32)

    @pl.loop(first, me + 1)
    def _(o):
        d = me - o
        gs = (sw_ref[d] * (dw_ref[d] - m_ref[...])).astype(BF16)
        total = dot_tn(gs, qs[...])
        acc[...] += dot_nn(gs, kbuf[o, cached:])
        gk_send[d] = total.astype(BF16)

        @pl.when(d == 0)
        def _():
            own_k[...] = total

        @pl.when(d > 0)
        def _():
            grad_copy(0, d, o).start()

    @pl.loop(0, n)
    def _(o):
        key = kbuf[o, 0:cached]
        for g in range(GROUP):
            w = s_ref[o, head(g)] * l_ref[head(g), 0:1]
            gs = (w * (dp_ref[o, head(g)] - m_ref[head(g), 0:1])).astype(BF16)
            acc[head(g)] += dot_nn(gs, key)

    for g in range(GROUP):
        dq_ref[:, g * HD : (g + 1) * HD] = (acc[head(g)] * scale).astype(BF16)

    @pl.loop(0, chips)
    def _(t):
        relay(0, t, "end")
        relay(1, t, "end")

    for k in range(1, n):
        pos_copy(me, (me + k) % n).wait_send()

    for d in range(1, rim + 1):
        @pl.when(me - d >= 0)
        def _():
            grad_copy(1, d, sib).wait_send()
            grad_copy(0, d, sib).wait_send()

        @pl.when(me + d < n)
        def _():
            grad_copy(1, d, sib).wait_recv()
            grad_copy(0, d, sib).wait_recv()
            own_k[...] += gk_recv[d].astype(F32)
            own_v[...] += gv_recv[d].astype(F32)

    dk_ref[...] = (own_k[...] * scale).astype(BF16)
    dv_ref[...] = own_v[...].astype(BF16)


def hand_over(*refs):
    count = len(refs) // 2
    sems = refs[-1]
    copies = [
        pltpu.make_async_copy(refs[i], refs[count + i], sems.at[i]) for i in range(count)
    ]
    for copy in copies:
        copy.start()
    for copy in copies:
        copy.wait()


def local(query, self_keys, self_values, cache_keys, cache_values, cache_pos, d_out):
    n = lax.axis_size("seq")
    rows = query.shape[0]
    cached = cache_keys.shape[0]
    rim = (WINDOW + rows - 2) // rows
    stacked = GROUP * rows
    vmem = pl.BlockSpec(memory_space=pltpu.VMEM)
    results = pl.pallas_call(
        functools.partial(kernel, n),
        out_shape=(
            jax.ShapeDtypeStruct((rows, GROUP * HD), BF16),
            jax.ShapeDtypeStruct((rows, GROUP * HD), BF16),
            jax.ShapeDtypeStruct((rows, HD), BF16),
            jax.ShapeDtypeStruct((rows, HD), BF16),
        ),
        in_specs=[vmem] * 7,
        out_specs=(vmem,) * 4,
        scratch_shapes=[
            pltpu.VMEM((stacked, HD), BF16),
            pltpu.VMEM((stacked, HD), BF16),
            pltpu.VMEM((n, cached + rows, HD), BF16),
            pltpu.VMEM((n, cached + rows, HD), BF16),
            pltpu.VMEM((n, 1, cached), jnp.int32),
            pltpu.VMEM((n, stacked, cached), F32),
            pltpu.VMEM((n, stacked, cached), F32),
            pltpu.VMEM((rim + 1, stacked, rows), F32),
            pltpu.VMEM((rim + 1, stacked, rows), F32),
            pltpu.VMEM((stacked, 128), F32),
            pltpu.VMEM((stacked, 128), F32),
            pltpu.VMEM((stacked, HD), F32),
            pltpu.VMEM((rows, HD), F32),
            pltpu.VMEM((rows, HD), F32),
            pltpu.VMEM((rim + 1, rows, HD), BF16),
            pltpu.VMEM((rim + 1, rows, HD), BF16),
            pltpu.VMEM((rim + 1, rows, HD), BF16),
            pltpu.VMEM((rim + 1, rows, HD), BF16),
            pltpu.SemaphoreType.DMA((2, 3, n)),
            pltpu.SemaphoreType.DMA((2, n)),
            pltpu.SemaphoreType.DMA((n,)),
            pltpu.SemaphoreType.DMA((n,)),
            pltpu.SemaphoreType.DMA((2, rim + 1)),
            pltpu.SemaphoreType.DMA((2, rim + 1)),
        ],
        compiler_params=pltpu.CompilerParams(
            collective_id=0, has_side_effects=True, vmem_limit_bytes=56 * 2**20
        ),
    )(
        query, self_keys, self_values, cache_keys, cache_values,
        cache_pos.reshape(1, cached), d_out,
    )
    anywhere = pl.BlockSpec(memory_space=pl.ANY)
    return pl.pallas_call(
        hand_over,
        out_shape=tuple(jax.ShapeDtypeStruct(x.shape, x.dtype) for x in results),
        in_specs=[anywhere] * len(results),
        out_specs=(anywhere,) * len(results),
        scratch_shapes=[pltpu.SemaphoreType.DMA((len(results),))],
    )(*results)


def solution(mesh):
    split = P(("batch", "seq"), "kvh")
    return jax.shard_map(
        local,
        mesh=mesh,
        in_specs=(split, split, split, split, split, P(("batch", "seq")), split),
        out_specs=(split, split, split, split),
        check_vma=False,
    )
```

```python
import functools
import math

import jax
import jax.numpy as jnp
from jax import lax
from jax.experimental import pallas as pl
from jax.experimental.pallas import tpu as pltpu
from jax.sharding import PartitionSpec as P

HD = 128
GROUP = 5
WINDOW = 512
NEG = -1e30
F32 = jnp.float32
BF16 = jnp.bfloat16
MESH = pl.DeviceIdType.MESH

LAST = (((1,), (1,)), ((), ()))
FIRST = (((0,), (0,)), ((), ()))


def dot_nt(a, b):
    return lax.dot_general(a, b, LAST, preferred_element_type=F32)


def dot_tn(a, b):
    return lax.dot_general(a, b, FIRST, preferred_element_type=F32)


def dot_nn(a, b):
    return jnp.dot(a, b, preferred_element_type=F32)


def lane_tiles(x, op):
    parts = [x[:, i : i + 128] for i in range(0, x.shape[1], 128)]
    return functools.reduce(op, parts)


def kernel(
    n, q_ref, sk_ref, sv_ref, ck_ref, cv_ref, cp_ref, do_ref,
    att_ref, dq_ref, dk_ref, dv_ref,
    qs, ds_out, kbuf, vbuf, pos, s_ref, dp_ref, sw_ref, dw_ref, m_ref, l_ref, acc, own_k, own_v,
    gk_send, gv_send, gk_recv, gv_recv,
    send_sem, recv_sem, pos_send, pos_recv, g_send, g_recv,
):
    rows = q_ref.shape[0]
    cached = ck_ref.shape[0]
    rim = (WINDOW + rows - 2) // rows
    rim_chips = (rim + 1) // 2
    chips = n // 2
    start_pos = (cached - rows) * n
    scale = HD ** -0.5
    scale2 = scale * math.log2(math.e)

    me = lax.axis_index("seq")
    z = me // 2
    core = me % 2
    sib = z * 2 + (1 - core)

    bufs = (kbuf, vbuf)
    kbuf[me, 0:cached] = ck_ref[...]
    kbuf[me, cached:] = sk_ref[...]
    vbuf[me, 0:cached] = cv_ref[...]
    vbuf[me, cached:] = sv_ref[...]
    pos[me] = cp_ref[...]

    barrier = pltpu.get_barrier_semaphore()
    for k in range(1, n):
        pl.semaphore_signal(
            barrier, inc=1, device_id={"seq": (me + k) % n}, device_id_type=MESH
        )
    pl.semaphore_wait(barrier, n - 1)

    def block_copy(a, way, o, size, target):
        part = bufs[a].at[o, pl.ds(0, size)]
        return pltpu.make_async_remote_copy(
            src_ref=part,
            dst_ref=part,
            send_sem=send_sem.at[a, way, o],
            recv_sem=recv_sem.at[a, o],
            device_id={"seq": target},
            device_id_type=MESH,
        )

    full = cached + rows

    def sized(near, run):
        @pl.when(near)
        def _():
            run(full)

        @pl.when(jnp.logical_not(near))
        def _():
            run(cached)

    def relay(a, t, act):
        left = me - 2 * t
        right = me + 2 * t

        def push(way, o, size, target):
            copy = block_copy(a, way, o, size, target)
            if act == "go":
                copy.start()
            else:
                copy.wait_send()

        @pl.when(z - t >= 0)
        def _():
            if act == "go":
                @pl.when(t > 0)
                def _():
                    sized(t <= rim_chips, lambda size: block_copy(a, 0, left, size, sib).wait_recv())

            @pl.when(z < chips - 1)
            def _():
                sized(t + 1 <= rim_chips, lambda size: push(0, left, size, me + 2))

            @pl.when(t == 0)
            def _():
                @pl.when(z > 0)
                def _():
                    push(1, left, cached, me - 2)

            sized(t <= rim_chips, lambda size: push(2, left, size, sib))

        @pl.when((t > 0) & (z + t < chips))
        def _():
            if act == "go":
                block_copy(a, 1, right, cached, sib).wait_recv()

            @pl.when(z > 0)
            def _():
                push(1, right, cached, me - 2)

            push(2, right, cached, sib)

    def consume(a, t, use):
        left = me - 2 * t
        right = me + 2 * t
        left_sib = left + sib - me
        right_sib = right + sib - me

        @pl.when(z - t >= 0)
        def _():
            use(left)

        @pl.when((t > 0) & (z + t < chips))
        def _():
            use(right)

        @pl.when(z - t >= 0)
        def _():
            sized(t <= rim_chips, lambda size: block_copy(a, 0, left_sib, size, sib).wait_recv())
            use(left_sib)

        @pl.when((t > 0) & (z + t < chips))
        def _():
            block_copy(a, 0, right_sib, cached, sib).wait_recv()
            use(right_sib)

    def pos_copy(o, target):
        return pltpu.make_async_remote_copy(
            src_ref=pos.at[o],
            dst_ref=pos.at[o],
            send_sem=pos_send.at[target],
            recv_sem=pos_recv.at[o],
            device_id={"seq": target},
            device_id_type=MESH,
        )

    relay(0, 0, "go")
    relay(1, 0, "go")
    for k in range(1, n):
        pos_copy(me, (me + k) % n).start()

    def head(g):
        return slice(g * rows, (g + 1) * rows)

    for g in range(GROUP):
        qs[head(g)] = q_ref[:, g * HD : (g + 1) * HD]
        ds_out[head(g)] = do_ref[:, g * HD : (g + 1) * HD]
    m_ref[...] = jnp.full(m_ref.shape, NEG, F32)
    l_ref[...] = jnp.zeros(l_ref.shape, F32)
    acc[...] = jnp.zeros(acc.shape, F32)

    row_index = me * rows + lax.broadcasted_iota(jnp.int32, (rows, 1), 0)
    bound = start_pos + jnp.maximum(row_index - WINDOW + 1, 0)

    def score_shard(o):
        @pl.when(o != me)
        def _():
            pos_copy(o, sib).wait_recv()

        vis = pos[o] < bound
        for g in range(GROUP):
            s = dot_nt(qs[head(g)], kbuf[o, 0:cached])
            s = jnp.where(vis, s, NEG)
            s_ref[o, head(g)] = s
            m_ref[head(g)] = jnp.maximum(m_ref[head(g)], lane_tiles(s, jnp.maximum))

    first = jnp.maximum(me - rim, 0)
    near_end = min(rim_chips, chips - 1)
    delta_index = lax.broadcasted_iota(jnp.int32, (rows, rows), 0) - lax.broadcasted_iota(
        jnp.int32, (rows, rows), 1
    )

    def window_scores():
        @pl.loop(first, me + 1)
        def _(o):
            d = me - o
            gap = delta_index + d * rows
            vis = (gap >= 0) & (gap < WINDOW)
            s = dot_nt(qs[...], kbuf[o, cached:])
            s = jnp.concatenate([jnp.where(vis, s[head(g)], NEG) for g in range(GROUP)], axis=0)
            sw_ref[d] = s
            m_ref[...] = jnp.maximum(m_ref[...], s)

    def window_values():
        @pl.loop(first, me + 1)
        def _(o):
            d = me - o
            v = vbuf[o, cached:]
            acc[...] += dot_nn(sw_ref[d].astype(BF16), v)
            dw_ref[d] = dot_nt(ds_out[...], v)

    @pl.loop(0, chips)
    def _(t):
        @pl.when(t > 0)
        def _():
            relay(0, t, "go")

        consume(0, t, score_shard)

        @pl.when(t > 0)
        def _():
            relay(1, t, "go")

        @pl.when(t == near_end)
        def _():
            window_scores()

    for g in range(GROUP):
        top = jnp.max(m_ref[head(g)], axis=1, keepdims=True)
        m_ref[head(g)] = jnp.broadcast_to(top, (rows, 128))

    @pl.loop(0, n)
    def _(o):
        for g in range(GROUP):
            p = jnp.exp2((s_ref[o, head(g)] - m_ref[head(g), 0:1]) * scale2)
            s_ref[o, head(g)] = p
            l_ref[head(g)] += lane_tiles(p, jnp.add)

    @pl.loop(first, me + 1)
    def _(o):
        d = me - o
        p = jnp.exp2((sw_ref[d] - m_ref[...]) * scale2)
        sw_ref[d] = p
        l_ref[...] += p

    for g in range(GROUP):
        total = jnp.sum(l_ref[head(g)], axis=1, keepdims=True)
        l_ref[head(g)] = jnp.broadcast_to(1.0 / total, (rows, 128))

    def grad_copy(a, d, target):
        sent, got = ((gk_send, gk_recv), (gv_send, gv_recv))[a]
        return pltpu.make_async_remote_copy(
            src_ref=sent.at[d],
            dst_ref=got.at[d],
            send_sem=g_send.at[a, d],
            recv_sem=g_recv.at[a, d],
            device_id={"seq": target},
            device_id_type=MESH,
        )

    @pl.loop(first, me + 1)
    def _(o):
        d = me - o
        w = sw_ref[d] * l_ref[...]
        sw_ref[d] = w
        total = dot_tn(w.astype(BF16), ds_out[...])
        gv_send[d] = total.astype(BF16)

        @pl.when(d == 0)
        def _():
            own_v[...] = total

        @pl.when(d > 0)
        def _():
            grad_copy(1, d, o).start()

    def value_shard(o):
        v = vbuf[o, 0:cached]
        for g in range(GROUP):
            w = s_ref[o, head(g)] * l_ref[head(g), 0:1]
            acc[head(g)] += dot_nn(w.astype(BF16), v)
            dp_ref[o, head(g)] = dot_nt(ds_out[head(g)], v)

    @pl.loop(0, chips)
    def _(t):
        consume(1, t, value_shard)

        @pl.when(t == near_end)
        def _():
            window_values()

    for g in range(GROUP):
        out = acc[head(g)].astype(BF16)
        att_ref[:, g * HD : (g + 1) * HD] = out
        delta = jnp.sum(ds_out[head(g)].astype(F32) * out.astype(F32), axis=1, keepdims=True)
        m_ref[head(g)] = jnp.broadcast_to(delta, (rows, 128))
    acc[...] = jnp.zeros(acc.shape, F32)

    @pl.loop(first, me + 1)
    def _(o):
        d = me - o
        gs = (sw_ref[d] * (dw_ref[d] - m_ref[...])).astype(BF16)
        total = dot_tn(gs, qs[...])
        acc[...] += dot_nn(gs, kbuf[o, cached:])
        gk_send[d] = total.astype(BF16)

        @pl.when(d == 0)
        def _():
            own_k[...] = total

        @pl.when(d > 0)
        def _():
            grad_copy(0, d, o).start()

    @pl.loop(0, n)
    def _(o):
        key = kbuf[o, 0:cached]
        for g in range(GROUP):
            w = s_ref[o, head(g)] * l_ref[head(g), 0:1]
            gs = (w * (dp_ref[o, head(g)] - m_ref[head(g), 0:1])).astype(BF16)
            acc[head(g)] += dot_nn(gs, key)

    for g in range(GROUP):
        dq_ref[:, g * HD : (g + 1) * HD] = (acc[head(g)] * scale).astype(BF16)

    @pl.loop(0, chips)
    def _(t):
        relay(0, t, "end")
        relay(1, t, "end")

    for k in range(1, n):
        pos_copy(me, (me + k) % n).wait_send()

    for d in range(1, rim + 1):
        @pl.when(me - d >= 0)
        def _():
            grad_copy(1, d, sib).wait_send()
            grad_copy(0, d, sib).wait_send()

        @pl.when(me + d < n)
        def _():
            grad_copy(1, d, sib).wait_recv()
            grad_copy(0, d, sib).wait_recv()
            own_k[...] += gk_recv[d].astype(F32)
            own_v[...] += gv_recv[d].astype(F32)

    dk_ref[...] = (own_k[...] * scale).astype(BF16)
    dv_ref[...] = own_v[...].astype(BF16)


def hand_over(*refs):
    count = len(refs) // 2
    for i in range(count):
        refs[count + i][...] = refs[i][...]


def local(query, self_keys, self_values, cache_keys, cache_values, cache_pos, d_out):
    n = lax.axis_size("seq")
    rows = query.shape[0]
    cached = cache_keys.shape[0]
    rim = (WINDOW + rows - 2) // rows
    stacked = GROUP * rows
    vmem = pl.BlockSpec(memory_space=pltpu.VMEM)
    results = pl.pallas_call(
        functools.partial(kernel, n),
        out_shape=(
            jax.ShapeDtypeStruct((rows, GROUP * HD), BF16),
            jax.ShapeDtypeStruct((rows, GROUP * HD), BF16),
            jax.ShapeDtypeStruct((rows, HD), BF16),
            jax.ShapeDtypeStruct((rows, HD), BF16),
        ),
        in_specs=[vmem] * 7,
        out_specs=(vmem,) * 4,
        scratch_shapes=[
            pltpu.VMEM((stacked, HD), BF16),
            pltpu.VMEM((stacked, HD), BF16),
            pltpu.VMEM((n, cached + rows, HD), BF16),
            pltpu.VMEM((n, cached + rows, HD), BF16),
            pltpu.VMEM((n, 1, cached), jnp.int32),
            pltpu.VMEM((n, stacked, cached), F32),
            pltpu.VMEM((n, stacked, cached), F32),
            pltpu.VMEM((rim + 1, stacked, rows), F32),
            pltpu.VMEM((rim + 1, stacked, rows), F32),
            pltpu.VMEM((stacked, 128), F32),
            pltpu.VMEM((stacked, 128), F32),
            pltpu.VMEM((stacked, HD), F32),
            pltpu.VMEM((rows, HD), F32),
            pltpu.VMEM((rows, HD), F32),
            pltpu.VMEM((rim + 1, rows, HD), BF16),
            pltpu.VMEM((rim + 1, rows, HD), BF16),
            pltpu.VMEM((rim + 1, rows, HD), BF16),
            pltpu.VMEM((rim + 1, rows, HD), BF16),
            pltpu.SemaphoreType.DMA((2, 3, n)),
            pltpu.SemaphoreType.DMA((2, n)),
            pltpu.SemaphoreType.DMA((n,)),
            pltpu.SemaphoreType.DMA((n,)),
            pltpu.SemaphoreType.DMA((2, rim + 1)),
            pltpu.SemaphoreType.DMA((2, rim + 1)),
        ],
        compiler_params=pltpu.CompilerParams(
            collective_id=0, has_side_effects=True, vmem_limit_bytes=56 * 2**20
        ),
    )(
        query, self_keys, self_values, cache_keys, cache_values,
        cache_pos.reshape(1, cached), d_out,
    )
    return pl.pallas_call(
        hand_over,
        out_shape=tuple(jax.ShapeDtypeStruct(x.shape, x.dtype) for x in results),
        in_specs=[vmem] * len(results),
        out_specs=(vmem,) * len(results),
    )(*results)


def solution(mesh):
    split = P(("batch", "seq"), "kvh")
    return jax.shard_map(
        local,
        mesh=mesh,
        in_specs=(split, split, split, split, split, P(("batch", "seq")), split),
        out_specs=(split, split, split, split),
        check_vma=False,
    )
```

```python
import functools
import math

import jax
import jax.numpy as jnp
from jax import lax
from jax.experimental import pallas as pl
from jax.experimental.pallas import tpu as pltpu
from jax.sharding import PartitionSpec as P

HD = 128
GROUP = 5
WINDOW = 512
NEG = -1e30
F32 = jnp.float32
BF16 = jnp.bfloat16
MESH = pl.DeviceIdType.MESH

LAST = (((1,), (1,)), ((), ()))
FIRST = (((0,), (0,)), ((), ()))


def dot_nt(a, b):
    return lax.dot_general(a, b, LAST, preferred_element_type=F32)


def dot_tn(a, b):
    return lax.dot_general(a, b, FIRST, preferred_element_type=F32)


def dot_nn(a, b):
    return jnp.dot(a, b, preferred_element_type=F32)


def lane_tiles(x, op):
    parts = [x[:, i : i + 128] for i in range(0, x.shape[1], 128)]
    return functools.reduce(op, parts)


def kernel(
    n, q_ref, sk_ref, sv_ref, ck_ref, cv_ref, cp_ref, do_ref,
    att_ref, dq_ref, dk_ref, dv_ref,
    qs, ds_out, kbuf, vbuf, pos, s_ref, dp_ref, sw_ref, dw_ref, m_ref, l_ref, acc, own_k, own_v,
    gk_send, gv_send, gk_recv, gv_recv,
    send_sem, recv_sem, pos_send, pos_recv, g_send, g_recv,
):
    rows = q_ref.shape[0]
    cached = ck_ref.shape[0]
    rim = (WINDOW + rows - 2) // rows
    rim_chips = (rim + 1) // 2
    chips = n // 2
    start_pos = (cached - rows) * n
    scale = HD ** -0.5
    scale2 = scale * math.log2(math.e)

    me = lax.axis_index("seq")
    z = me // 2
    core = me % 2
    sib = z * 2 + (1 - core)

    bufs = (kbuf, vbuf)
    kbuf[me, 0:cached] = ck_ref[...]
    kbuf[me, cached:] = sk_ref[...]
    vbuf[me, 0:cached] = cv_ref[...]
    vbuf[me, cached:] = sv_ref[...]
    pos[me] = cp_ref[...]

    barrier = pltpu.get_barrier_semaphore()
    for k in range(1, n):
        pl.semaphore_signal(
            barrier, inc=1, device_id={"seq": (me + k) % n}, device_id_type=MESH
        )
    pl.semaphore_wait(barrier, n - 1)

    def block_copy(a, way, o, size, target):
        part = bufs[a].at[o, pl.ds(0, size)]
        return pltpu.make_async_remote_copy(
            src_ref=part,
            dst_ref=part,
            send_sem=send_sem.at[a, way, o],
            recv_sem=recv_sem.at[a, o],
            device_id={"seq": target},
            device_id_type=MESH,
        )

    full = cached + rows

    def sized(near, run):
        @pl.when(near)
        def _():
            run(full)

        @pl.when(jnp.logical_not(near))
        def _():
            run(cached)

    def relay(a, t, act):
        left = me - 2 * t
        right = me + 2 * t

        def push(way, o, size, target):
            copy = block_copy(a, way, o, size, target)
            if act == "go":
                copy.start()
            else:
                copy.wait_send()

        @pl.when(z - t >= 0)
        def _():
            if act == "go":
                @pl.when(t > 0)
                def _():
                    sized(t <= rim_chips, lambda size: block_copy(a, 0, left, size, sib).wait_recv())

            @pl.when(z < chips - 1)
            def _():
                sized(t + 1 <= rim_chips, lambda size: push(0, left, size, me + 2))

            @pl.when(t == 0)
            def _():
                @pl.when(z > 0)
                def _():
                    push(1, left, cached, me - 2)

            sized(t <= rim_chips, lambda size: push(2, left, size, sib))

        @pl.when((t > 0) & (z + t < chips))
        def _():
            if act == "go":
                block_copy(a, 1, right, cached, sib).wait_recv()

            @pl.when(z > 0)
            def _():
                push(1, right, cached, me - 2)

            push(2, right, cached, sib)

    def consume(a, t, use):
        left = me - 2 * t
        right = me + 2 * t
        left_sib = left + sib - me
        right_sib = right + sib - me

        @pl.when(z - t >= 0)
        def _():
            use(left)

        @pl.when((t > 0) & (z + t < chips))
        def _():
            use(right)

        @pl.when(z - t >= 0)
        def _():
            sized(t <= rim_chips, lambda size: block_copy(a, 0, left_sib, size, sib).wait_recv())
            use(left_sib)

        @pl.when((t > 0) & (z + t < chips))
        def _():
            block_copy(a, 0, right_sib, cached, sib).wait_recv()
            use(right_sib)

    def pos_copy(o, target):
        return pltpu.make_async_remote_copy(
            src_ref=pos.at[o],
            dst_ref=pos.at[o],
            send_sem=pos_send.at[target],
            recv_sem=pos_recv.at[o],
            device_id={"seq": target},
            device_id_type=MESH,
        )

    relay(0, 0, "go")
    relay(1, 0, "go")
    for k in range(1, n):
        pos_copy(me, (me + k) % n).start()

    def head(g):
        return slice(g * rows, (g + 1) * rows)

    for g in range(GROUP):
        qs[head(g)] = q_ref[:, g * HD : (g + 1) * HD]
        ds_out[head(g)] = do_ref[:, g * HD : (g + 1) * HD]
    m_ref[...] = jnp.full(m_ref.shape, NEG, F32)
    l_ref[...] = jnp.zeros(l_ref.shape, F32)
    acc[...] = jnp.zeros(acc.shape, F32)

    row_index = me * rows + lax.broadcasted_iota(jnp.int32, (rows, 1), 0)
    bound = start_pos + jnp.maximum(row_index - WINDOW + 1, 0)

    def score_shard(o):
        @pl.when(o != me)
        def _():
            pos_copy(o, sib).wait_recv()

        vis = pos[o] < bound
        for g in range(GROUP):
            s = dot_nt(qs[head(g)], kbuf[o, 0:cached])
            s = jnp.where(vis, s, NEG)
            s_ref[o, head(g)] = s
            m_ref[head(g)] = jnp.maximum(m_ref[head(g)], lane_tiles(s, jnp.maximum))

    first = jnp.maximum(me - rim, 0)
    near_end = min(rim_chips, chips - 1)
    delta_index = lax.broadcasted_iota(jnp.int32, (rows, rows), 0) - lax.broadcasted_iota(
        jnp.int32, (rows, rows), 1
    )

    def window_scores():
        @pl.loop(first, me + 1)
        def _(o):
            d = me - o
            gap = delta_index + d * rows
            vis = (gap >= 0) & (gap < WINDOW)
            s = dot_nt(qs[...], kbuf[o, cached:])
            s = jnp.concatenate([jnp.where(vis, s[head(g)], NEG) for g in range(GROUP)], axis=0)
            sw_ref[d] = s
            m_ref[...] = jnp.maximum(m_ref[...], s)

    def window_values():
        @pl.loop(first, me + 1)
        def _(o):
            d = me - o
            v = vbuf[o, cached:]
            acc[...] += dot_nn(sw_ref[d].astype(BF16), v)
            dw_ref[d] = dot_nt(ds_out[...], v)

    @pl.loop(0, chips)
    def _(t):
        @pl.when(t > 0)
        def _():
            relay(0, t, "go")

        consume(0, t, score_shard)

        @pl.when((t > 0) & (t < chips - 1))
        def _():
            relay(1, t, "go")

        @pl.when(t == near_end)
        def _():
            window_scores()

    for g in range(GROUP):
        top = jnp.max(m_ref[head(g)], axis=1, keepdims=True)
        m_ref[head(g)] = jnp.broadcast_to(top, (rows, 128))

    @pl.loop(0, n)
    def _(o):
        for g in range(GROUP):
            p = jnp.exp2((s_ref[o, head(g)] - m_ref[head(g), 0:1]) * scale2)
            s_ref[o, head(g)] = p
            l_ref[head(g)] += lane_tiles(p, jnp.add)

    @pl.loop(first, me + 1)
    def _(o):
        d = me - o
        p = jnp.exp2((sw_ref[d] - m_ref[...]) * scale2)
        sw_ref[d] = p
        l_ref[...] += p

    for g in range(GROUP):
        total = jnp.sum(l_ref[head(g)], axis=1, keepdims=True)
        l_ref[head(g)] = jnp.broadcast_to(1.0 / total, (rows, 128))

    def grad_copy(a, d, target):
        sent, got = ((gk_send, gk_recv), (gv_send, gv_recv))[a]
        return pltpu.make_async_remote_copy(
            src_ref=sent.at[d],
            dst_ref=got.at[d],
            send_sem=g_send.at[a, d],
            recv_sem=g_recv.at[a, d],
            device_id={"seq": target},
            device_id_type=MESH,
        )

    @pl.loop(first, me + 1)
    def _(o):
        d = me - o
        w = sw_ref[d] * l_ref[...]
        sw_ref[d] = w
        total = dot_tn(w.astype(BF16), ds_out[...])
        gv_send[d] = total.astype(BF16)

        @pl.when(d == 0)
        def _():
            own_v[...] = total

        @pl.when(d > 0)
        def _():
            grad_copy(1, d, o).start()

    def value_shard(o):
        v = vbuf[o, 0:cached]
        for g in range(GROUP):
            w = s_ref[o, head(g)] * l_ref[head(g), 0:1]
            acc[head(g)] += dot_nn(w.astype(BF16), v)
            dp_ref[o, head(g)] = dot_nt(ds_out[head(g)], v)

    @pl.loop(0, chips)
    def _(t):
        @pl.when(t == chips - 1)
        def _():
            relay(1, t, "go")

        consume(1, t, value_shard)

        @pl.when(t == near_end)
        def _():
            window_values()

    for g in range(GROUP):
        out = acc[head(g)].astype(BF16)
        att_ref[:, g * HD : (g + 1) * HD] = out
        delta = jnp.sum(ds_out[head(g)].astype(F32) * out.astype(F32), axis=1, keepdims=True)
        m_ref[head(g)] = jnp.broadcast_to(delta, (rows, 128))
    acc[...] = jnp.zeros(acc.shape, F32)

    @pl.loop(first, me + 1)
    def _(o):
        d = me - o
        gs = (sw_ref[d] * (dw_ref[d] - m_ref[...])).astype(BF16)
        total = dot_tn(gs, qs[...])
        acc[...] += dot_nn(gs, kbuf[o, cached:])
        gk_send[d] = total.astype(BF16)

        @pl.when(d == 0)
        def _():
            own_k[...] = total

        @pl.when(d > 0)
        def _():
            grad_copy(0, d, o).start()

    @pl.loop(0, n)
    def _(o):
        key = kbuf[o, 0:cached]
        for g in range(GROUP):
            w = s_ref[o, head(g)] * l_ref[head(g), 0:1]
            gs = (w * (dp_ref[o, head(g)] - m_ref[head(g), 0:1])).astype(BF16)
            acc[head(g)] += dot_nn(gs, key)

    for g in range(GROUP):
        dq_ref[:, g * HD : (g + 1) * HD] = (acc[head(g)] * scale).astype(BF16)

    @pl.loop(0, chips)
    def _(t):
        relay(0, t, "end")
        relay(1, t, "end")

    for k in range(1, n):
        pos_copy(me, (me + k) % n).wait_send()

    for d in range(1, rim + 1):
        @pl.when(me - d >= 0)
        def _():
            grad_copy(1, d, sib).wait_send()
            grad_copy(0, d, sib).wait_send()

        @pl.when(me + d < n)
        def _():
            grad_copy(1, d, sib).wait_recv()
            grad_copy(0, d, sib).wait_recv()
            own_k[...] += gk_recv[d].astype(F32)
            own_v[...] += gv_recv[d].astype(F32)

    dk_ref[...] = (own_k[...] * scale).astype(BF16)
    dv_ref[...] = own_v[...].astype(BF16)


def hand_over(*refs):
    count = len(refs) // 2
    for i in range(count):
        refs[count + i][...] = refs[i][...]


def local(query, self_keys, self_values, cache_keys, cache_values, cache_pos, d_out):
    n = lax.axis_size("seq")
    rows = query.shape[0]
    cached = cache_keys.shape[0]
    rim = (WINDOW + rows - 2) // rows
    stacked = GROUP * rows
    vmem = pl.BlockSpec(memory_space=pltpu.VMEM)
    results = pl.pallas_call(
        functools.partial(kernel, n),
        out_shape=(
            jax.ShapeDtypeStruct((rows, GROUP * HD), BF16),
            jax.ShapeDtypeStruct((rows, GROUP * HD), BF16),
            jax.ShapeDtypeStruct((rows, HD), BF16),
            jax.ShapeDtypeStruct((rows, HD), BF16),
        ),
        in_specs=[vmem] * 7,
        out_specs=(vmem,) * 4,
        scratch_shapes=[
            pltpu.VMEM((stacked, HD), BF16),
            pltpu.VMEM((stacked, HD), BF16),
            pltpu.VMEM((n, cached + rows, HD), BF16),
            pltpu.VMEM((n, cached + rows, HD), BF16),
            pltpu.VMEM((n, 1, cached), jnp.int32),
            pltpu.VMEM((n, stacked, cached), F32),
            pltpu.VMEM((n, stacked, cached), F32),
            pltpu.VMEM((rim + 1, stacked, rows), F32),
            pltpu.VMEM((rim + 1, stacked, rows), F32),
            pltpu.VMEM((stacked, 128), F32),
            pltpu.VMEM((stacked, 128), F32),
            pltpu.VMEM((stacked, HD), F32),
            pltpu.VMEM((rows, HD), F32),
            pltpu.VMEM((rows, HD), F32),
            pltpu.VMEM((rim + 1, rows, HD), BF16),
            pltpu.VMEM((rim + 1, rows, HD), BF16),
            pltpu.VMEM((rim + 1, rows, HD), BF16),
            pltpu.VMEM((rim + 1, rows, HD), BF16),
            pltpu.SemaphoreType.DMA((2, 3, n)),
            pltpu.SemaphoreType.DMA((2, n)),
            pltpu.SemaphoreType.DMA((n,)),
            pltpu.SemaphoreType.DMA((n,)),
            pltpu.SemaphoreType.DMA((2, rim + 1)),
            pltpu.SemaphoreType.DMA((2, rim + 1)),
        ],
        compiler_params=pltpu.CompilerParams(
            collective_id=0, has_side_effects=True, vmem_limit_bytes=56 * 2**20
        ),
    )(
        query, self_keys, self_values, cache_keys, cache_values,
        cache_pos.reshape(1, cached), d_out,
    )
    return pl.pallas_call(
        hand_over,
        out_shape=tuple(jax.ShapeDtypeStruct(x.shape, x.dtype) for x in results),
        in_specs=[vmem] * len(results),
        out_specs=(vmem,) * len(results),
    )(*results)


def solution(mesh):
    split = P(("batch", "seq"), "kvh")
    return jax.shard_map(
        local,
        mesh=mesh,
        in_specs=(split, split, split, split, split, P(("batch", "seq")), split),
        out_specs=(split, split, split, split),
        check_vma=False,
    )
```
